512 devices in a mesh: queue: 64 (over x_lo, z, core), space: 8 (over y, x_hi).
Axes of the slice: x: 4 (x_hi: 2, x_lo: 2; x = x_hi * 2 + x_lo), y: 4, z: 16, core: 2. Of those that a mesh axis runs over, the one named last changes fastest.
Arguments:
- hidden: bfloat16 [64, 192, 3072], P('queue', 'space')
- qkv_weight: bfloat16 [3, 3072, 2048], P(None, 'queue', 'space'), may hold values from -0.109375 to 0.109375
- out_weight: bfloat16 [3072, 2048], P('queue', 'space'), may hold values from -0.125 to 0.125
- mod_weight: bfloat16 [256, 3, 3072], P(None, None, 'space'), may hold values from -0.375 to 0.375
- slot_frame: int32 [64], replicated, may hold values from 0 to 63, as said below
- levels: int32 [64], replicated, may hold values from 2 to 11, as said below
- timesteps: int32 [12], replicated, may hold values from 40 to 996, as said below
Outputs:
- velocity: bfloat16 [2, 64, 192, 3072], P(None, 'queue', 'space')
- latents: bfloat16 [64, 192, 3072], P('queue', 'space')
The draws below stay inside these ranges and needn't reach their ends.
Inputs may be any that keep to these rules, and one draw needn't show every extreme that they name: `slot_frame`: slot q holds frame (q - r) mod 64 for one r of the draw. `levels`: never falling from frame to frame; frame 0 has level 2 and the last frame level 11. `timesteps`: strictly rising.
All inputs are finite; a program needn't handle non-finite values.
Results may differ from the reference program's by a relative error of at most 0.023.
Values may be sent and summed in bfloat16 or wider, within the bound.
A program may use at most 64 MiB of HBM per device.

```python
import math
import jax
import jax.numpy as jnp
from jax import lax

D = 3072
HEADS = 16
HEAD_DIM = 128
FREQ = 256
WINDOW = 16
STEPS = 2
NUM_LEVELS = 12
FRAMES = 64
SPATIAL = 192
INNER = 2048
N_SPACE = 8


def draw_hidden(key, part):
    key = jax.random.fold_in(key, 11)
    key_rows, key_cols, key_body = jax.random.split(key, 3)
    row_scale = jnp.exp(jax.random.uniform(key_rows, (FRAMES, SPATIAL, 1), jnp.float32, math.log(0.3), math.log(3.0)))
    col_scale = jnp.exp(jax.random.uniform(key_cols, (1, 1, D), jnp.float32, math.log(0.3), math.log(3.0)))
    values = jax.random.normal(key_body, (FRAMES, SPATIAL, D), jnp.float32)
    return (0.06 * values * row_scale * col_scale).astype(jnp.bfloat16)


def draw_slot_frame(key, part):
    key = jax.random.fold_in(key, 12)
    rotation = jax.random.randint(key, (), 0, FRAMES)
    return ((jnp.arange(FRAMES) - rotation) % FRAMES).astype(jnp.int32)


def draw_levels(key, part):
    key = jax.random.fold_in(key, 13)
    middle = jax.random.randint(key, (FRAMES - 2,), STEPS, NUM_LEVELS)
    first_level = jnp.full((1,), STEPS, jnp.int32)
    last_level = jnp.full((1,), NUM_LEVELS - 1, jnp.int32)
    return jnp.sort(jnp.concatenate([first_level, middle.astype(jnp.int32), last_level])).astype(jnp.int32)


def draw_timesteps(key, part):
    key = jax.random.fold_in(key, 14)
    increments = jax.random.randint(key, (NUM_LEVELS - 2,), 40, 84)
    inner = 40 + jnp.cumsum(increments)
    first_step = jnp.full((1,), 40, jnp.int32)
    last_step = jnp.full((1,), 83 * NUM_LEVELS, jnp.int32)
    return jnp.concatenate([first_step, inner.astype(jnp.int32), last_step]).astype(jnp.int32)


def steps_of(stream_key, dims, cuts, least, top_value):
    def one(dim, blocks):
        draws = jax.random.uniform(jax.random.fold_in(jax.random.fold_in(stream_key, 6), dim), (blocks,), jnp.float32, least / len(cuts), top_value / len(cuts))
        return jnp.repeat(jnp.exp(draws), dims[dim] // blocks).reshape((-1,) + (1,) * (len(dims) - dim - 1))

    gain = one(*cuts[0])
    for cut in cuts[1:]:
        gain = gain * one(*cut)
    return gain


def centred(stream_key, dims, spread, limit, cuts=(), kind=jnp.bfloat16):
    level = steps_of(stream_key, dims, cuts, -0.22, 0.18) if cuts else 1.0
    values = jax.random.normal(stream_key, dims, jnp.float32) * spread * level
    return jnp.minimum(jnp.maximum(values, -limit), limit).astype(kind)


def setup_inputs(seed: int = 0) -> dict:
    keys = jax.random.split(jax.random.key(seed), 8)
    hidden = draw_hidden(jax.random.fold_in(keys[7], 71), 0)
    qkv_weight = centred(keys[1], (3, D, INNER), D ** -0.5, 0.109375, ((1, 64), (2, 8)))
    out_weight = centred(keys[2], (D, INNER), INNER ** -0.5, 0.125, ((0, 64), (1, 8)))
    mod_weight = centred(keys[3], (FREQ, 3, D), FREQ ** -0.5, 0.375, ((2, 8),))
    slot_frame = draw_slot_frame(jax.random.fold_in(keys[7], 71), 0)
    levels = draw_levels(jax.random.fold_in(keys[7], 71), 0)
    timesteps = draw_timesteps(jax.random.fold_in(keys[7], 71), 0)
    return dict(hidden=hidden, qkv_weight=qkv_weight, out_weight=out_weight, mod_weight=mod_weight, slot_frame=slot_frame, levels=levels, timesteps=timesteps)


def embed_time(t_now):
    half_freq = FREQ // 2
    omega = jnp.exp(-math.log(10000.0) * jnp.arange(half_freq).astype(jnp.float32) / half_freq)
    angles = t_now[:, None] * omega[None, :]
    return jnp.concatenate([jnp.cos(angles), jnp.sin(angles)], axis=-1).astype(jnp.bfloat16)

def rms_heads(values):
    wide = values.astype(jnp.float32)
    return (wide / jnp.sqrt(lax.optimization_barrier(jnp.mean(wide * wide, axis=-1, keepdims=True)) + 1e-06)).astype(jnp.bfloat16)

def reference(hidden, qkv_weight, out_weight, mod_weight, slot_frame, levels, timesteps):
    half_window = WINDOW // 2
    offsets = jnp.arange(-half_window, half_window).astype(jnp.int32)
    target = slot_frame[:, None] + offsets[None, :]
    valid = ((target >= 0) & (target < FRAMES)).astype(jnp.float32)
    groups = N_SPACE
    group_width = INNER // groups
    weight_groups = out_weight.astype(jnp.float32).reshape(D, groups, group_width).transpose(1, 0, 2)
    state = hidden
    outputs = []
    for step_index in range(STEPS):
        level_now = levels[slot_frame] - step_index
        t_now = timesteps[level_now].astype(jnp.float32)
        t_next = timesteps[level_now - 1].astype(jnp.float32)
        sigma_step = (t_next - t_now) / 1000.0
        embedding = embed_time(t_now)
        modulation = jnp.einsum('qf,fkd->qkd', embedding.astype(jnp.float32), mod_weight.astype(jnp.float32))
        mod_shift = modulation[:, 0][:, None, :]
        mod_scale = modulation[:, 1][:, None, :]
        mod_gate = modulation[:, 2][:, None, :]
        current = state.astype(jnp.float32)
        row_mean = lax.optimization_barrier(jnp.mean(current, axis=-1, keepdims=True))
        centered = current - row_mean
        row_var = lax.optimization_barrier(jnp.mean(centered * centered, axis=-1, keepdims=True))
        normed = (centered / jnp.sqrt(row_var + 1e-06) * (1.0 + mod_scale) + mod_shift).astype(jnp.bfloat16)
        projected = jnp.einsum('qsd,kdc->qskc', normed.astype(jnp.float32), qkv_weight.astype(jnp.float32)).astype(jnp.bfloat16)
        shape_heads = (FRAMES, SPATIAL, HEADS, HEAD_DIM)
        query_hat = rms_heads(projected[:, :, 0].reshape(shape_heads)).astype(jnp.float32)
        key_hat = rms_heads(projected[:, :, 1].reshape(shape_heads)).astype(jnp.float32)
        value_all = projected[:, :, 2].reshape(shape_heads).astype(jnp.float32)
        score_list = []
        for offset in range(-half_window, half_window):
            rolled = jnp.roll(key_hat, -offset, axis=0)
            score_list.append(jnp.einsum('qshc,qshc->qsh', query_hat, rolled) / math.sqrt(HEAD_DIM))
        scores = jnp.stack(score_list)
        expo = jnp.exp(scores) * valid.T[:, :, None, None]
        attn_weights = (expo / lax.optimization_barrier(jnp.sum(expo, axis=0, keepdims=True))).astype(jnp.bfloat16).astype(jnp.float32)
        attended = jnp.zeros(shape_heads, jnp.float32)
        for index, offset in enumerate(range(-half_window, half_window)):
            rolled = jnp.roll(value_all, -offset, axis=0)
            attended = attended + attn_weights[index][..., None] * rolled
        attended = attended.astype(jnp.bfloat16).reshape(FRAMES, SPATIAL, groups, group_width).astype(jnp.float32)

        def add_group(carry, group_index):
            part_in = lax.dynamic_index_in_dim(attended, group_index, 2, keepdims=False)
            part_w = lax.dynamic_index_in_dim(weight_groups, group_index, 0, keepdims=False)
            partial_sum = jnp.einsum('qsc,dc->qsd', part_in, part_w).astype(jnp.bfloat16)
            partial_sum = lax.optimization_barrier(partial_sum)
            return (carry + partial_sum.astype(jnp.float32), None)
        branch, unused = lax.scan(add_group, jnp.zeros((FRAMES, SPATIAL, D), jnp.float32), jnp.arange(groups).astype(jnp.int32))
        velocity_now = current + mod_gate * branch
        outputs.append(velocity_now.astype(jnp.bfloat16))
        state = (current + sigma_step[:, None, None] * velocity_now).astype(jnp.bfloat16)
    return (jnp.stack(outputs), state)
```

```python
import functools
import math

import jax
import jax.numpy as jnp
from jax import lax
from jax.experimental import pallas as pl
from jax.experimental.pallas import tpu as pltpu
from jax.sharding import PartitionSpec as P

MESH = pl.DeviceIdType.MESH
F32 = jnp.float32
BF16 = jnp.bfloat16
HEAD_DIM = 128
FREQ = 256
STEPS = 2
GROUPS = 3
HALF = 1536
SPACE = 8
FRAMES = 64


def kernel(
    hid, qkvw, outw, modw, omega, slot_frame, levels, timesteps,
    vel_out, lat_out,
    W, XS, MP, MG, MODF, G, LHS, KV, QS, ATT, PB, RB, VO,
    w_send, z_recv, x_recv, sib_recv, mod_send, mod_recv,
    ag_send, ag_recv, rs_send, rs_recv, kv_send, kv_recv, kvs_recv,
):
    q = lax.axis_index("queue")
    me = lax.axis_index("space")
    xl = q // 32
    z = (q % 32) // 2
    c = q % 2
    sib = q + 1 - 2 * c
    xp = (q + 32) % FRAMES

    def zq(d):
        return xl * 32 + ((z + d + 16) % 16) * 2 + c

    def xzq(d):
        return (1 - xl) * 32 + ((z + d + 16) % 16) * 2 + c

    up_q = (q + 2) % FRAMES
    down_q = (q + FRAMES - 2) % FRAMES
    peers = [(me + k) % SPACE for k in range(1, SPACE)]

    def send(src, dst, ss, rs, dev):
        pltpu.make_async_remote_copy(
            src_ref=src, dst_ref=dst, send_sem=ss, recv_sem=rs,
            device_id=dev, device_id_type=MESH,
        ).start()

    def wait(ref, sem):
        pltpu.make_async_copy(ref, ref, sem).wait()

    barrier = pltpu.get_barrier_semaphore()
    targets = [(zq(1), me), (zq(-1), me), (xp, me), (sib, me), (up_q, me), (down_q, me)]
    targets += [(q, p) for p in peers]
    for dev in targets:
        pl.semaphore_signal(barrier, inc=1, device_id=dev, device_id_type=MESH)

    W[q, 0] = qkvw[1]
    W[q, 1] = qkvw[2]
    W[q, 2] = qkvw[0]
    W[q, 3] = outw[...]

    frame = slot_frame[q]
    level = levels[frame]
    t_a = timesteps[level].astype(F32)
    t_b = timesteps[jnp.maximum(level - 1, 0)].astype(F32)
    t_c = timesteps[jnp.maximum(level - 2, 0)].astype(F32)
    dsigma = [(t_b - t_a) * (1.0 / 1000.0), (t_c - t_b) * (1.0 / 1000.0)]

    row = lax.broadcasted_iota(jnp.int32, (16, FREQ // 2), 0)
    angle = jnp.where(row % 2 == 0, t_a, t_b) * omega[...]
    emb = jnp.concatenate([jnp.cos(angle), jnp.sin(angle)], axis=-1).astype(BF16)
    cols = SPACE * 48
    part = [
        jnp.dot(emb, modw[k], preferred_element_type=F32)[:8] for k in range(3)
    ]
    prow = lax.broadcasted_iota(jnp.int32, (8, cols), 0)
    packed = jnp.where(prow < 2, part[0], jnp.where(prow < 4, part[1], part[2]))
    MP[...] = packed
    MG[me] = packed

    x = hid[0].astype(F32)
    for g in range(GROUPS):
        XS[g, 0] = x[8 * g : 8 * g + 8, :HALF]
        XS[g, 1] = x[8 * g : 8 * g + 8, HALF:]

    pl.semaphore_wait(barrier, len(targets))

    kv_half, qo_half = pl.ds(0, 2), pl.ds(2, 2)

    def w_move(idx, half, rs, dev):
        send(W.at[idx, half], W.at[idx, half], w_send, rs, dev)

    up, down = (zq(1), me), (zq(-1), me)
    xdev, sdev = (xp, me), (sib, me)
    w_move(q, kv_half, x_recv.at[16], xdev)
    w_move(q, kv_half, z_recv.at[0, 0, 0], up)
    w_move(q, kv_half, z_recv.at[1, 0, 0], down)
    w_move(q, qo_half, z_recv.at[0, 0, 2], up)
    w_move(q, qo_half, z_recv.at[1, 0, 2], down)
    w_move(q, kv_half, sib_recv.at[0], sdev)
    for p in peers:
        send(MP, MG.at[me], mod_send, mod_recv, (q, p))
    w_move(q, qo_half, x_recv.at[0], xdev)
    w_move(q, qo_half, sib_recv.at[1], sdev)

    wait(W.at[xp, kv_half], x_recv.at[16])
    w_move(xp, kv_half, z_recv.at[0, 0, 1], up)
    w_move(xp, kv_half, z_recv.at[1, 0, 1], down)
    w_move(xp, kv_half, sib_recv.at[0], sdev)

    def relay(h, way):
        d = -h if way == 0 else h
        onward = up if way == 0 else down
        own, other = zq(d), xzq(d)
        last = h == 8
        for m in (0, 1, 2):
            if last and ((m == 1) == (way == 0)):
                continue
            idx = other if m == 1 else own
            half = qo_half if m == 2 else kv_half
            wait(W.at[idx, half], z_recv.at[way, h - 1, m])
            more = h < 7 or (h == 7 and (m == 1) == (way == 1))
            if more:
                w_move(idx, half, z_recv.at[way, h, m], onward)
            if m == 2:
                w_move(idx, half, x_recv.at[h if way == 0 else 8 + h], xdev)
            w_move(idx, half, sib_recv.at[1 if m == 2 else 0], sdev)

    def take_x(j):
        idx = xp if j == 0 else (xzq(-j) if j <= 8 else xzq(j - 8))
        wait(W.at[idx, qo_half], x_recv.at[j])
        w_move(idx, qo_half, sib_recv.at[1], sdev)

    def spread_modulation():
        wait(MG.at[pl.ds(0, SPACE - 1)], mod_recv)
        for st in range(STEPS):
            for k in range(3):
                r = 2 * k + st
                for half in range(2):
                    vec = jnp.concatenate(
                        [MG[4 * half + j, r : r + 1, :] for j in range(4)], axis=-1
                    )
                    if k == 1:
                        vec = vec + 1.0
                    MODF[st, k, half] = jnp.broadcast_to(vec, (8, HALF))

    def norm_send(st, g):
        left, right = XS[g, 0], XS[g, 1]
        mean = (
            jnp.sum(left, axis=-1, keepdims=True) + jnp.sum(right, axis=-1, keepdims=True)
        ) * (1.0 / (2 * HALF))
        left, right = left - mean, right - mean
        var = (
            jnp.sum(left * left, axis=-1, keepdims=True)
            + jnp.sum(right * right, axis=-1, keepdims=True)
        ) * (1.0 / (2 * HALF))
        inv = 1.0 / jnp.sqrt(var + 1e-6)
        left = left * inv * MODF[st, 1, 0] + MODF[st, 0, 0]
        right = right * inv * MODF[st, 1, 1] + MODF[st, 0, 1]
        G[st, g, me] = jnp.concatenate([left, right], axis=0).astype(BF16)
        for p in peers:
            send(G.at[st, g, me], G.at[st, g, me], ag_send.at[st, g], ag_recv.at[st, g], (q, p))

    def rms(values):
        parts = []
        for h in range(2):
            wide = values[:, h * HEAD_DIM : (h + 1) * HEAD_DIM]
            mean = jnp.mean(wide * wide, axis=-1, keepdims=True)
            parts.append(wide * (1.0 / jnp.sqrt(mean + 1e-6)))
        return jnp.concatenate(parts, axis=-1)

    def project(g, part_index):
        acc = None
        for j in range(4):
            term = jnp.dot(
                LHS[g, :, 768 * j : 768 * (j + 1)],
                W[16 * j : 16 * (j + 1), part_index].reshape(768, 256),
                preferred_element_type=F32,
            )
            acc = term if acc is None else acc + term
        return acc.astype(BF16)

    def kv_move(st, g, w, rs, dev, to):
        send(KV.at[st, g, w], KV.at[st, g, to], kv_send.at[st, g], rs, dev)

    def sib_kv(st, g, w):
        to = w + 2 * c - 1
        kv_move(st, g, w, kvs_recv.at[st, g, to], sdev, to)

    kv_up, kv_down = (up_q, me), (down_q, me)

    def take_rows(st, g):
        wait(G.at[st, g, pl.ds(0, SPACE - 1)], ag_recv.at[st, g])
        rows = G[st, g].astype(F32)
        LHS[g, :, :HALF] = rows[:, :8].reshape(64, HALF).astype(BF16)
        LHS[g, :, HALF:] = rows[:, 8:].reshape(64, HALF).astype(BF16)

    def project_kv(st, g):
        KV[st, g, 8, 0] = rms(project(g, 0).astype(F32)).astype(BF16)
        KV[st, g, 8, 1] = project(g, 1)
        kv_move(st, g, 8, kv_recv.at[st, g, 3], kv_up, 6)
        kv_move(st, g, 8, kv_recv.at[st, g, 5], kv_down, 10)
        sib_kv(st, g, 8)

    def project_q(st, g):
        hat = rms(project(g, 2).astype(F32)).astype(BF16).astype(F32)
        QS[g] = hat * (1.0 / math.sqrt(HEAD_DIM))

    def kv_relay(st, g, h):
        lo, hi = 8 - 2 * h, 8 + 2 * h
        wait(KV.at[st, g, lo], kv_recv.at[st, g, lo // 2])
        if h < 4:
            kv_move(st, g, lo, kv_recv.at[st, g, lo // 2 - 1], kv_up, lo - 2)
            sib_kv(st, g, lo)
            wait(KV.at[st, g, hi], kv_recv.at[st, g, hi // 2])
            if h < 3:
                kv_move(st, g, hi, kv_recv.at[st, g, hi // 2 + 1], kv_down, hi + 2)
            else:

                @pl.when(c == 0)
                def _():
                    kv_move(st, g, hi, kv_recv.at[st, g, hi // 2 + 1], kv_down, hi + 2)

            sib_kv(st, g, hi)
        else:

            @pl.when(c == 0)
            def _():
                wait(KV.at[st, g, hi], kv_recv.at[st, g, hi // 2])
                sib_kv(st, g, hi)

            @pl.when(c == 1)
            def _():
                sib_kv(st, g, lo)

    masks = []
    for w in range(16):
        f = frame + (w - 8)
        masks.append(jnp.where((f >= 0) & (f < FRAMES), 1.0, 0.0).astype(F32))

    def attend(st, g):
        for w in range(1, 16, 2):
            wait(KV.at[st, g, w], kvs_recv.at[st, g, w])

        def rows16(i, carry):
            at = pl.ds(pl.multiple_of(i * 16, 16), 16)
            for h in range(2):
                lanes = pl.ds(h * HEAD_DIM, HEAD_DIM)
                query = QS[g, at, lanes]
                num = jnp.zeros((16, HEAD_DIM), F32)
                den = jnp.zeros((16, 1), F32)
                for w in range(16):
                    key = KV[st, g, w, 0, at, lanes].astype(F32)
                    score = jnp.sum(query * key, axis=-1, keepdims=True)
                    e = jnp.exp(score) * masks[w]
                    den = den + e
                    num = num + e * KV[st, g, w, 1, at, lanes].astype(F32)
                ATT[g, at, lanes] = (num / den).astype(BF16)
            return carry

        lax.fori_loop(0, 4, rows16, 0)

    def out_send(st, g):
        for j in range(2):
            pair = []
            for half in range(2):
                k = j + 2 * half
                pair.append(
                    lax.dot_general(
                        ATT[g],
                        W[16 * k : 16 * (k + 1), 3].reshape(768, 256),
                        (((1,), (1,)), ((), ())),
                        preferred_element_type=F32,
                    ).reshape(8, 8, 768)
                )
            PB[st, g, :, :, 768 * j : 768 * (j + 1)] = jnp.concatenate(pair, axis=1).astype(BF16)
        RB[st, g, me] = PB[st, g, me]
        for p in peers:
            send(PB.at[st, g, p], RB.at[st, g, me], rs_send.at[st, g], rs_recv.at[st, g], (q, p))

    def update(st, g):
        wait(RB.at[st, g, pl.ds(0, SPACE - 1)], rs_recv.at[st, g])
        branch = jnp.sum(RB[st, g].astype(F32), axis=0)
        for half in range(2):
            cur = XS[g, half]
            vel = cur + MODF[st, 2, half] * branch[8 * half : 8 * half + 8]
            VO[st, 8 * g : 8 * g + 8, half * HALF : (half + 1) * HALF] = vel
            XS[g, half] = (cur + dsigma[st] * vel).astype(BF16).astype(F32)

    spread_modulation()
    for g in range(GROUPS):
        norm_send(0, g)
    for h in range(1, 9):
        relay(h, 0)
        relay(h, 1)
        if h == 1:
            take_x(0)
        else:
            take_x(h - 1)
            take_x(8 + h - 1)
    take_x(8)
    wait(W.at[pl.ds(0, 32), kv_half], sib_recv.at[0])
    wait(W.at[pl.ds(0, 32), qo_half], sib_recv.at[1])

    for st in range(STEPS):
        for g in range(GROUPS):
            take_rows(st, g)
            project_kv(st, g)
        for g in range(GROUPS):
            project_q(st, g)
        for h in range(1, 4):
            for g in range(GROUPS):
                kv_relay(st, g, h)
        kv_relay(st, 0, 4)
        kv_relay(st, 1, 4)
        attend(st, 0)
        out_send(st, 0)
        kv_relay(st, 2, 4)
        attend(st, 1)
        out_send(st, 1)
        attend(st, 2)
        out_send(st, 2)
        for g in range(GROUPS):
            update(st, g)
            if st + 1 < STEPS:
                norm_send(st + 1, g)

    for st in range(STEPS):
        vel_out[st, 0] = VO[st].astype(BF16)
    for g in range(GROUPS):
        for half in range(2):
            VO[0, 8 * g : 8 * g + 8, half * HALF : (half + 1) * HALF] = XS[g, half]
    lat_out[0] = VO[0].astype(BF16)

    wait(W.at[pl.ds(0, 63)], w_send)
    wait(MG.at[pl.ds(0, SPACE - 1)], mod_send)
    for st in range(STEPS):
        for g in range(GROUPS):
            wait(G.at[st, g, pl.ds(0, SPACE - 1)], ag_send.at[st, g])
            wait(RB.at[st, g, pl.ds(0, SPACE - 1)], rs_send.at[st, g])

            @pl.when(c == 0)
            def _():
                wait(KV.at[st, g, pl.ds(0, 16)], kv_send.at[st, g])

            @pl.when(c == 1)
            def _():
                wait(KV.at[st, g, pl.ds(0, 15)], kv_send.at[st, g])


def shards(hidden, qkv_weight, out_weight, mod_weight, slot_frame, levels, timesteps):
    half_freq = FREQ // 2
    omega = jnp.exp(-math.log(10000.0) * jnp.arange(half_freq).astype(F32) / half_freq)
    vmem = pl.BlockSpec(memory_space=pltpu.VMEM)
    smem = pl.BlockSpec(memory_space=pltpu.SMEM)
    dma = pltpu.SemaphoreType.DMA
    width = SPACE * 48
    return pl.pallas_call(
        kernel,
        name="denoise",
        out_shape=(
            jax.ShapeDtypeStruct((STEPS, 1, 24, 2 * HALF), BF16),
            jax.ShapeDtypeStruct((1, 24, 2 * HALF), BF16),
        ),
        in_specs=[vmem] * 5 + [smem] * 3,
        out_specs=(vmem, vmem),
        scratch_shapes=[
            pltpu.VMEM((FRAMES, 4, 48, 256), BF16),
            pltpu.VMEM((GROUPS, 2, 8, HALF), F32),
            pltpu.VMEM((8, width), F32),
            pltpu.VMEM((SPACE, 8, width), F32),
            pltpu.VMEM((STEPS, 3, 2, 8, HALF), F32),
            pltpu.VMEM((STEPS, GROUPS, SPACE, 16, HALF), BF16),
            pltpu.VMEM((GROUPS, 64, 2 * HALF), BF16),
            pltpu.VMEM((STEPS, GROUPS, 17, 2, 64, 256), BF16),
            pltpu.VMEM((GROUPS, 64, 256), F32),
            pltpu.VMEM((GROUPS, 64, 256), BF16),
            pltpu.VMEM((STEPS, GROUPS, SPACE, 16, HALF), BF16),
            pltpu.VMEM((STEPS, GROUPS, SPACE, 16, HALF), BF16),
            pltpu.VMEM((STEPS, 24, 2 * HALF), F32),
            dma,
            dma((2, 8, 3)),
            dma((17,)),
            dma((2,)),
            dma,
            dma,
            dma((STEPS, GROUPS)),
            dma((STEPS, GROUPS)),
            dma((STEPS, GROUPS)),
            dma((STEPS, GROUPS)),
            dma((STEPS, GROUPS)),
            dma((STEPS, GROUPS, 9)),
            dma((STEPS, GROUPS, 16)),
        ],
        compiler_params=pltpu.CompilerParams(
            collective_id=0, has_side_effects=True, vmem_limit_bytes=48 * 1024 * 1024
        ),
    )(
        hidden, qkv_weight, out_weight, jnp.transpose(mod_weight, (1, 0, 2)), omega[None],
        slot_frame, levels, timesteps,
    )


def solution(mesh):
    in_specs = (
        P("queue", "space", None),
        P(None, "queue", "space"),
        P("queue", "space"),
        P(None, None, "space"),
        P(),
        P(),
        P(),
    )
    out_specs = (P(None, "queue", "space", None), P("queue", "space", None))
    return jax.shard_map(shards, mesh=mesh, in_specs=in_specs, out_specs=out_specs, check_vma=False)
```

```python
import functools
import math

import jax
import jax.numpy as jnp
from jax import lax
from jax.experimental import pallas as pl
from jax.experimental.pallas import tpu as pltpu
from jax.sharding import PartitionSpec as P

MESH = pl.DeviceIdType.MESH
F32 = jnp.float32
BF16 = jnp.bfloat16
HEAD_DIM = 128
FREQ = 256
STEPS = 2
GROUPS = 3
HALF = 1536
SPACE = 8
FRAMES = 64


def kernel(
    hid, qkvw, outw, modw, omega, slot_frame, levels, timesteps,
    vel_out, lat_out,
    W, WX, XS, MP, MG, MODF, G, LHS, KV, QS, ATT, ATX, PB, RB, VO, HS, MW, in_sem,
    w_send, z_recv, x_recv, sib_recv, wx_send, wx_recv, mod_send, mod_recv,
    ag_send, ag_recv, agx_recv, agy_recv, at_send, at_recv, rs_send, rs_recv,
    kv_send, kv_recv, kvs_recv,
):
    q = lax.axis_index("queue")
    me = lax.axis_index("space")
    xl = q // 32
    z = (q % 32) // 2
    c = q % 2
    y, xh = me // 2, me % 2
    slot = xh * 4 + y
    sib = q + 1 - 2 * c
    xp = (q + 32) % FRAMES

    def zq(d):
        return xl * 32 + ((z + d + 16) % 16) * 2 + c

    def xzq(d):
        return (1 - xl) * 32 + ((z + d + 16) % 16) * 2 + c

    up_q = (q + 2) % FRAMES
    down_q = (q + FRAMES - 2) % FRAMES
    peers = [(me + k) % SPACE for k in range(1, SPACE)]
    ydevs = [(q, (me + 2 * k) % SPACE) for k in (1, 3, 2)]
    hdev = (q, me + 1 - 2 * xh)
    odev = (xp, me + 1 - 2 * xh)
    kv_up, kv_down = (up_q, me), (down_q, me)
    up, down = (zq(1), me), (zq(-1), me)
    xdev, sdev = (xp, me), (sib, me)

    def send(src, dst, ss, rs, dev):
        pltpu.make_async_remote_copy(
            src_ref=src, dst_ref=dst, send_sem=ss, recv_sem=rs,
            device_id=dev, device_id_type=MESH,
        ).start()

    def wait(ref, sem):
        pltpu.make_async_copy(ref, ref, sem).wait()

    barrier = pltpu.get_barrier_semaphore()
    targets = [up, down, xdev, sdev, odev, kv_up, kv_down] + [(q, p) for p in peers]
    for dev in targets:
        pl.semaphore_signal(barrier, inc=1, device_id=dev, device_id_type=MESH)

    loads = [
        pltpu.make_async_copy(qkvw.at[pl.ds(1, 2)], W.at[q // 2, c, pl.ds(0, 2)], in_sem.at[0]),
        pltpu.make_async_copy(qkvw.at[0], W.at[q // 2, c, 2], in_sem.at[1]),
        pltpu.make_async_copy(outw, W.at[q // 2, c, 3], in_sem.at[2]),
        pltpu.make_async_copy(modw, MW, in_sem.at[3]),
        pltpu.make_async_copy(hid.at[0], HS, in_sem.at[4]),
    ]
    for load in loads:
        load.start()

    kv_half, qo_half = pl.ds(0, 2), pl.ds(2, 2)

    def w_move(idx, half, rs, dev):
        ref = W.at[idx // 2, c, half]
        send(ref, ref, w_send.at[1 if dev is sdev else 0], rs, dev)

    def w_wait(idx, half, sem):
        wait(W.at[idx // 2, c, half], sem)

    def z_move(idx, k, h, way, m):
        w_move(idx, k, z_recv.at[way, h, m], down if way else up)

    for load in loads[:3]:
        load.wait()
    pl.semaphore_wait(barrier, len(targets))
    z_move(q, 0, 0, 0, 0)
    z_move(q, 0, 0, 1, 0)
    w_move(q, kv_half, x_recv.at[16], xdev)
    z_move(q, 1, 0, 0, 1)
    z_move(q, 1, 0, 1, 1)
    for k in (2, 3):
        z_move(q, k, 0, 0, k + 2)
        z_move(q, k, 0, 1, k + 2)
    w_move(q, qo_half, x_recv.at[0], xdev)
    w_move(q, kv_half, sib_recv.at[0], sdev)
    w_move(q, qo_half, sib_recv.at[1], sdev)

    frame = slot_frame[q]
    level = levels[frame]
    t_a = timesteps[level].astype(F32)
    t_b = timesteps[jnp.maximum(level - 1, 0)].astype(F32)
    t_c = timesteps[jnp.maximum(level - 2, 0)].astype(F32)
    dsigma = [(t_b - t_a) * (1.0 / 1000.0), (t_c - t_b) * (1.0 / 1000.0)]

    row = lax.broadcasted_iota(jnp.int32, (16, FREQ // 2), 0)
    angle = jnp.where(row % 2 == 0, t_a, t_b) * omega[...]
    emb = jnp.concatenate([jnp.cos(angle), jnp.sin(angle)], axis=-1).astype(BF16)
    cols = SPACE * 48
    loads[3].wait()
    part = [
        jnp.dot(emb, MW[k], preferred_element_type=F32)[:8] for k in range(3)
    ]
    prow = lax.broadcasted_iota(jnp.int32, (8, cols), 0)
    packed = jnp.where(prow < 2, part[0], jnp.where(prow < 4, part[1], part[2]))
    MP[...] = packed
    MG[me] = packed
    for p in peers:
        send(MP, MG.at[me], mod_send, mod_recv, (q, p))

    loads[4].wait()
    x = HS[...].astype(F32)
    for g in range(GROUPS):
        XS[g, 0] = x[8 * g : 8 * g + 8, :HALF]
        XS[g, 1] = x[8 * g : 8 * g + 8, HALF:]

    def seed():
        w_wait(xp, kv_half, x_recv.at[16])
        for k in (0, 1):
            z_move(xp, k, 0, 0, k + 2)
            z_move(xp, k, 0, 1, k + 2)
        w_move(xp, kv_half, sib_recv.at[0], sdev)

    def relay(h, way, m):
        theirs = m in (2, 3)
        if h == 8 and theirs == (way == 0):
            return
        d = -h if way == 0 else h
        idx = xzq(d) if theirs else zq(d)
        k = (0, 1, 0, 1, 2, 3)[m]
        w_wait(idx, k, z_recv.at[way, h - 1, m])
        if h < 7 or (h == 7 and theirs == (way == 1)):
            z_move(idx, k, h, way, m)
        if m % 2 == 1:
            half = qo_half if m == 5 else kv_half
            if m == 5:
                w_move(idx, half, x_recv.at[h if way == 0 else 8 + h], xdev)
            w_move(idx, half, sib_recv.at[1 if m == 5 else 0], sdev)

    def take_x(j):
        idx = xp if j == 0 else (xzq(-j) if j <= 8 else xzq(j - 8))
        w_wait(idx, qo_half, x_recv.at[j])
        w_move(idx, qo_half, sib_recv.at[1], sdev)

    def finish_weights():
        wait(W.at[pl.ds(0, 16), pl.ds(0, 2), qo_half], sib_recv.at[1])

    def partner_weights():
        send(W.at[pl.ds(0, 32), c, 3], WX.at[pl.ds(0, 32), c], wx_send.at[0], wx_recv.at[0], odev)

    def share_partner_weights():
        own = WX.at[pl.ds(0, 32), c]
        wait(own, wx_recv.at[0])
        send(own, own, wx_send.at[1], wx_recv.at[1], sdev)

    def finish_partner_weights():
        wait(WX.at[pl.ds(0, 32), c], wx_recv.at[1])

    def spread_modulation():
        wait(MG.at[pl.ds(0, SPACE - 1)], mod_recv)
        for st in range(STEPS):
            for k in range(3):
                r = 2 * k + st
                for half in range(2):
                    vec = jnp.concatenate(
                        [MG[4 * half + j, r : r + 1, :] for j in range(4)], axis=-1
                    )
                    if k == 1:
                        vec = vec + 1.0
                    MODF[st, k, half] = jnp.broadcast_to(vec, (8, HALF))

    def g_move(st, g, at, rs, dev):
        ref = G.at[st, g, at]
        send(ref, ref, ag_send.at[st, g], rs, dev)

    def norm_send(st, g):
        left, right = XS[g, 0], XS[g, 1]
        mean = (
            jnp.sum(left, axis=-1, keepdims=True) + jnp.sum(right, axis=-1, keepdims=True)
        ) * (1.0 / (2 * HALF))
        left, right = left - mean, right - mean
        var = (
            jnp.sum(left * left, axis=-1, keepdims=True)
            + jnp.sum(right * right, axis=-1, keepdims=True)
        ) * (1.0 / (2 * HALF))
        inv = 1.0 / jnp.sqrt(var + 1e-6)
        left = left * inv * MODF[st, 1, 0] + MODF[st, 0, 0]
        right = right * inv * MODF[st, 1, 1] + MODF[st, 0, 1]
        G[st, g, slot] = jnp.concatenate([left, right], axis=0).astype(BF16)
        g_move(st, g, slot, agx_recv.at[st, g], hdev)
        g_move(st, g, slot, ag_recv.at[st, g], ydevs[0])
        g_move(st, g, slot, ag_recv.at[st, g], ydevs[1])
        g_move(st, g, slot, agy_recv.at[st, g], ydevs[2])

    def norm_pass(st, g):
        other = (1 - xh) * 4 + y
        wait(G.at[st, g, other], agx_recv.at[st, g])
        g_move(st, g, other, ag_recv.at[st, g], ydevs[0])
        g_move(st, g, other, ag_recv.at[st, g], ydevs[1])
        far = xh * 4 + (y + 2) % 4
        wait(G.at[st, g, far], agy_recv.at[st, g])
        g_move(st, g, far, ag_recv.at[st, g], hdev)

    def rms(values):
        parts = []
        for h in range(2):
            wide = values[:, h * HEAD_DIM : (h + 1) * HEAD_DIM]
            mean = jnp.mean(wide * wide, axis=-1, keepdims=True)
            parts.append(wide * (1.0 / jnp.sqrt(mean + 1e-6)))
        return jnp.concatenate(parts, axis=-1)

    def project(g, part_index):
        acc = None
        for j in range(4):
            term = jnp.dot(
                LHS[g, :, 768 * j : 768 * (j + 1)],
                W[8 * j : 8 * (j + 1), :, part_index].reshape(768, 256),
                preferred_element_type=F32,
            )
            acc = term if acc is None else acc + term
        return acc.astype(BF16)

    def kv_move(st, g, w, k, rs, dev, to):
        send(KV.at[st, g, w, k], KV.at[st, g, to, k], kv_send.at[st, g], rs, dev)

    def kv_pass(st, g, w, k, way):
        to = w + 2 if way else w - 2
        kv_move(st, g, w, k, kv_recv.at[st, g, to // 2, k], kv_down if way else kv_up, to)

    def kv_wait(st, g, w, k):
        wait(KV.at[st, g, w, k], kv_recv.at[st, g, w // 2, k])

    def sib_kv(st, g, w):
        to = w + 2 * c - 1
        send(KV.at[st, g, w], KV.at[st, g, to], kv_send.at[st, g], kvs_recv.at[st, g, to], sdev)

    def take_rows(st, g):
        wait(G.at[st, g, pl.ds(0, 5)], ag_recv.at[st, g])
        rows = G[st, g].astype(F32)
        LHS[g, :, :HALF] = rows[:, :8].reshape(64, HALF).astype(BF16)
        LHS[g, :, HALF:] = rows[:, 8:].reshape(64, HALF).astype(BF16)

    def project_kv(st, g):
        KV[st, g, 8, 0] = rms(project(g, 0).astype(F32)).astype(BF16)
        kv_pass(st, g, 8, 0, 0)
        kv_pass(st, g, 8, 0, 1)
        KV[st, g, 8, 1] = project(g, 1)
        kv_pass(st, g, 8, 1, 0)
        kv_pass(st, g, 8, 1, 1)
        sib_kv(st, g, 8)

    def project_q(st, g):
        hat = rms(project(g, 2).astype(F32)).astype(BF16).astype(F32)
        QS[g] = hat * (1.0 / math.sqrt(HEAD_DIM))

    def kv_relay(st, g, h):
        lo, hi = 8 - 2 * h, 8 + 2 * h
        if h < 4:
            for k in range(2):
                kv_wait(st, g, lo, k)
                kv_pass(st, g, lo, k, 0)
                kv_wait(st, g, hi, k)
                if h < 3:
                    kv_pass(st, g, hi, k, 1)
                else:

                    @pl.when(c == 0)
                    def _():
                        kv_pass(st, g, hi, k, 1)

            sib_kv(st, g, lo)
            sib_kv(st, g, hi)
        else:
            kv_wait(st, g, lo, 0)
            kv_wait(st, g, lo, 1)

            @pl.when(c == 0)
            def _():
                kv_wait(st, g, hi, 0)
                kv_wait(st, g, hi, 1)
                sib_kv(st, g, hi)

            @pl.when(c == 1)
            def _():
                sib_kv(st, g, lo)

    masks = []
    for w in range(16):
        f = frame + (w - 8)
        masks.append(jnp.where((f >= 0) & (f < FRAMES), 1.0, 0.0).astype(F32))

    def attend(st, g):
        for w in range(1, 16, 2):
            wait(KV.at[st, g, w], kvs_recv.at[st, g, w])

        def rows16(i, carry):
            at = pl.ds(pl.multiple_of(i * 16, 16), 16)
            for h in range(2):
                lanes = pl.ds(h * HEAD_DIM, HEAD_DIM)
                query = QS[g, at, lanes]
                num = jnp.zeros((16, HEAD_DIM), F32)
                den = jnp.zeros((16, 1), F32)
                for w in range(16):
                    key = KV[st, g, w, 0, at, lanes].astype(F32)
                    score = jnp.sum(query * key, axis=-1, keepdims=True)
                    e = jnp.exp(score) * masks[w]
                    den = den + e
                    num = num + e * KV[st, g, w, 1, at, lanes].astype(F32)
                ATT[st, g, i // 2, pl.ds(pl.multiple_of((i % 2) * 16, 16), 16), lanes] = (
                    num / den
                ).astype(BF16)
            return carry

        lax.fori_loop(0, 4, rows16, 0)
        send(ATT.at[st, g, 1 - xh], ATX.at[st, g], at_send.at[st, g], at_recv.at[st, g], hdev)

    def out_send(st, g):
        wait(ATX.at[st, g], at_recv.at[st, g])
        own, other = ATT[st, g, xh], ATX[st, g]
        for j in range(2):
            pair = []
            for half in range(2):
                k = j + 2 * half
                total = None
                for rows, weight in (
                    (own, W[8 * k : 8 * (k + 1), :, 3]), (other, WX[8 * k : 8 * (k + 1)])
                ):
                    term = lax.dot_general(
                        rows, weight.reshape(768, 256), (((1,), (1,)), ((), ())),
                        preferred_element_type=F32,
                    )
                    total = term if total is None else total + term
                pair.append(total.reshape(4, 8, 768))
            PB[st, g, :, :, 768 * j : 768 * (j + 1)] = jnp.concatenate(pair, axis=1).astype(BF16)
        RB[st, g, y] = PB[st, g, y]
        for k, dev in zip((1, 3, 2), ydevs):
            send(
                PB.at[st, g, (y + k) % 4], RB.at[st, g, y],
                rs_send.at[st, g], rs_recv.at[st, g], dev,
            )

    def update(st, g):
        wait(RB.at[st, g, pl.ds(0, 3)], rs_recv.at[st, g])
        branch = jnp.sum(RB[st, g].astype(F32), axis=0)
        for half in range(2):
            cur = XS[g, half]
            vel = cur + MODF[st, 2, half] * branch[8 * half : 8 * half + 8]
            VO[st, 8 * g : 8 * g + 8, half * HALF : (half + 1) * HALF] = vel
            XS[g, half] = (cur + dsigma[st] * vel).astype(BF16).astype(F32)

    for h in range(1, 9):
        for m in range(6):
            relay(h, 0, m)
            relay(h, 1, m)
            if h == 1 and m == 1:
                seed()
        if h == 1:
            take_x(0)
            spread_modulation()
        else:
            take_x(h - 1)
            take_x(8 + h - 1)
        if 2 <= h <= 4:
            norm_send(0, h - 2)
        if 5 <= h <= 7:
            norm_pass(0, h - 5)
    take_x(8)
    partner_weights()
    wait(W.at[pl.ds(0, 16), pl.ds(0, 2), kv_half], sib_recv.at[0])

    for st in range(STEPS):
        for g in range(GROUPS):
            take_rows(st, g)
            project_kv(st, g)
        if st == 0:
            finish_weights()
        for g in range(GROUPS):
            project_q(st, g)
        for h in range(1, 4):
            for g in range(GROUPS):
                kv_relay(st, g, h)
        if st == 0:
            share_partner_weights()
        else:
            vel_out[0, 0] = VO[0].astype(BF16)
        kv_relay(st, 0, 4)
        kv_relay(st, 1, 4)
        attend(st, 0)
        kv_relay(st, 2, 4)
        attend(st, 1)
        if st == 0:
            finish_partner_weights()
        out_send(st, 0)
        attend(st, 2)
        out_send(st, 1)
        out_send(st, 2)
        for g in range(GROUPS):
            update(st, g)
            if st + 1 < STEPS:
                norm_send(st + 1, g)
                if g > 0:
                    norm_pass(st + 1, g - 1)
        if st + 1 < STEPS:
            norm_pass(st + 1, GROUPS - 1)

    vel_out[1, 0] = VO[1].astype(BF16)
    for g in range(GROUPS):
        for half in range(2):
            VO[0, 8 * g : 8 * g + 8, half * HALF : (half + 1) * HALF] = XS[g, half]
    lat_out[0] = VO[0].astype(BF16)

    wait(W.at[pl.ds(0, 31), 0], w_send.at[0])
    wait(W.at[pl.ds(0, 16)], w_send.at[1])
    for k in range(2):
        wait(WX.at[pl.ds(0, 32), c], wx_send.at[k])
    wait(MG.at[pl.ds(0, SPACE - 1)], mod_send)
    for st in range(STEPS):
        for g in range(GROUPS):
            wait(G.at[st, g, pl.ds(0, SPACE - 1)], ag_send.at[st, g])
            wait(ATX.at[st, g], at_send.at[st, g])
            wait(RB.at[st, g, pl.ds(0, 3)], rs_send.at[st, g])

            @pl.when(c == 0)
            def _():
                wait(KV.at[st, g, pl.ds(0, 16)], kv_send.at[st, g])

            @pl.when(c == 1)
            def _():
                wait(KV.at[st, g, pl.ds(0, 15)], kv_send.at[st, g])


def shards(hidden, qkv_weight, out_weight, mod_weight, slot_frame, levels, timesteps):
    half_freq = FREQ // 2
    omega = jnp.exp(-math.log(10000.0) * jnp.arange(half_freq).astype(F32) / half_freq)
    vmem = pl.BlockSpec(memory_space=pltpu.VMEM)
    hbm = pl.BlockSpec(memory_space=pltpu.HBM)
    smem = pl.BlockSpec(memory_space=pltpu.SMEM)
    dma = pltpu.SemaphoreType.DMA
    width = SPACE * 48
    return pl.pallas_call(
        kernel,
        name="denoise",
        out_shape=(
            jax.ShapeDtypeStruct((STEPS, 1, 24, 2 * HALF), BF16),
            jax.ShapeDtypeStruct((1, 24, 2 * HALF), BF16),
        ),
        in_specs=[hbm] * 4 + [vmem] + [smem] * 3,
        out_specs=(vmem, vmem),
        scratch_shapes=[
            pltpu.VMEM((FRAMES // 2, 2, 4, 48, 256), BF16),
            pltpu.VMEM((FRAMES // 2, 2, 48, 256), BF16),
            pltpu.VMEM((GROUPS, 2, 8, HALF), F32),
            pltpu.VMEM((8, width), F32),
            pltpu.VMEM((SPACE, 8, width), F32),
            pltpu.VMEM((STEPS, 3, 2, 8, HALF), F32),
            pltpu.VMEM((STEPS, GROUPS, SPACE, 16, HALF), BF16),
            pltpu.VMEM((GROUPS, 64, 2 * HALF), BF16),
            pltpu.VMEM((STEPS, GROUPS, 17, 2, 64, 256), BF16),
            pltpu.VMEM((GROUPS, 64, 256), F32),
            pltpu.VMEM((STEPS, GROUPS, 2, 32, 256), BF16),
            pltpu.VMEM((STEPS, GROUPS, 32, 256), BF16),
            pltpu.VMEM((STEPS, GROUPS, 4, 16, HALF), BF16),
            pltpu.VMEM((STEPS, GROUPS, 4, 16, HALF), BF16),
            pltpu.VMEM((STEPS, 24, 2 * HALF), F32),
            pltpu.VMEM((24, 2 * HALF), BF16),
            pltpu.VMEM((3, FREQ, width), BF16),
            dma((5,)),
            dma((2,)),
            dma((2, 8, 6)),
            dma((17,)),
            dma((2,)),
            dma((2,)),
            dma((2,)),
            dma,
            dma,
            dma((STEPS, GROUPS)),
            dma((STEPS, GROUPS)),
            dma((STEPS, GROUPS)),
            dma((STEPS, GROUPS)),
            dma((STEPS, GROUPS)),
            dma((STEPS, GROUPS)),
            dma((STEPS, GROUPS)),
            dma((STEPS, GROUPS)),
            dma((STEPS, GROUPS)),
            dma((STEPS, GROUPS, 9, 2)),
            dma((STEPS, GROUPS, 16)),
        ],
        compiler_params=pltpu.CompilerParams(
            collective_id=0, has_side_effects=True, vmem_limit_bytes=63 * 1024 * 1024
        ),
    )(
        hidden, qkv_weight, out_weight, jnp.transpose(mod_weight, (1, 0, 2)), omega[None],
        slot_frame, levels, timesteps,
    )


def solution(mesh):
    in_specs = (
        P("queue", "space", None),
        P(None, "queue", "space"),
        P("queue", "space"),
        P(None, None, "space"),
        P(),
        P(),
        P(),
    )
    out_specs = (P(None, "queue", "space", None), P("queue", "space", None))
    return jax.shard_map(shards, mesh=mesh, in_specs=in_specs, out_specs=out_specs, check_vma=False)
```

```python
import functools
import math

import jax
import jax.numpy as jnp
import numpy as np
from jax import lax
from jax.experimental import pallas as pl
from jax.experimental.pallas import tpu as pltpu
from jax.sharding import PartitionSpec as P

MESH = pl.DeviceIdType.MESH
F32 = jnp.float32
BF16 = jnp.bfloat16
HEAD_DIM = 128
FREQ = 256
STEPS = 2
GROUPS = 3
HALF = 1536
SPACE = 8
ORDER = [("near", 0), ("near", 1), ("near", 2), (4, 0), (4, 1), (4, 2), ("share", 0), ("far", 0), ("far", 1),
         ("shared", 0), ("far", 2), ("out", 0), ("out", 1), ("out", 2)]
X_TURNS = {h: [] for h in range(1, 10)}
for _j in range(16):
    X_TURNS[(max(1, _j if _j <= 8 else _j - 8) + 1) if _j else 1].append(_j)
FRAMES = 64
FAR = (0, 1, 15)
NEAR = tuple(w for w in range(16) if w not in FAR)


def kernel(
    hid, qkvw, outw, modw, omega, slot_frame, levels, timesteps,
    vel_out, lat_out,
    W, WX, XS, MP, MG, MODF, G, LHS, KV, QS, NUM, DEN, ATT, ATX, PB, RB, VO, HS, MW, OM, in_sem,
    w_send, z_recv, x_recv, sib_recv, wx_send, wx_recv, mod_send, mod_recv,
    ag_send, ag_recv, agx_recv, agy_recv, at_send, at_recv, rs_send, rs_recv,
    kv_send, kv_recv, kvs_recv,
):
    q = lax.axis_index("queue")
    me = lax.axis_index("space")
    xl = q // 32
    z = (q % 32) // 2
    c = q % 2
    y, xh = me // 2, me % 2
    slot = xh * 4 + y
    sib = q + 1 - 2 * c
    xp = (q + 32) % FRAMES

    def zq(d):
        return xl * 32 + ((z + d + 16) % 16) * 2 + c

    def xzq(d):
        return (1 - xl) * 32 + ((z + d + 16) % 16) * 2 + c

    up_q = (q + 2) % FRAMES
    down_q = (q + FRAMES - 2) % FRAMES
    peers = [(me + k) % SPACE for k in range(1, SPACE)]
    ydevs = [(q, (me + 2 * k) % SPACE) for k in (1, 3, 2)]
    hdev = (q, me + 1 - 2 * xh)
    odev = (xp, me + 1 - 2 * xh)
    kv_up, kv_down = (up_q, me), (down_q, me)
    up, down = (zq(1), me), (zq(-1), me)
    xdev, sdev = (xp, me), (sib, me)

    def send(src, dst, ss, rs, dev):
        pltpu.make_async_remote_copy(
            src_ref=src, dst_ref=dst, send_sem=ss, recv_sem=rs,
            device_id=dev, device_id_type=MESH,
        ).start()

    def wait(ref, sem):
        pltpu.make_async_copy(ref, ref, sem).wait()

    barrier = pltpu.get_barrier_semaphore()
    targets = [up, down, xdev, sdev, odev, kv_up, kv_down] + [(q, p) for p in peers]
    for dev in targets:
        pl.semaphore_signal(barrier, inc=1, device_id=dev, device_id_type=MESH)

    loads = [
        pltpu.make_async_copy(qkvw.at[pl.ds(1, 2)], W.at[q // 2, c, pl.ds(0, 2)], in_sem.at[0]),
        pltpu.make_async_copy(qkvw.at[0], W.at[q // 2, c, 2], in_sem.at[1]),
        pltpu.make_async_copy(outw, W.at[q // 2, c, 3], in_sem.at[2]),
        pltpu.make_async_copy(modw, MW, in_sem.at[3]),
        pltpu.make_async_copy(hid.at[0], HS, in_sem.at[4]),
        pltpu.make_async_copy(omega, OM, in_sem.at[5]),
    ]
    for load in loads:
        load.start()

    kv_half, qo_half = pl.ds(0, 2), pl.ds(2, 2)

    def w_move(idx, half, rs, dev):
        ref = W.at[idx // 2, c, half]
        send(ref, ref, w_send.at[1 if dev is sdev else 0], rs, dev)

    def w_wait(idx, half, sem):
        wait(W.at[idx // 2, c, half], sem)

    def z_move(idx, k, h, way, m):
        w_move(idx, k, z_recv.at[way, h, m], down if way else up)

    for load in loads[:3]:
        load.wait()
    pl.semaphore_wait(barrier, len(targets))
    z_move(q, 0, 0, 0, 0)
    z_move(q, 0, 0, 1, 0)
    w_move(q, kv_half, x_recv.at[16], xdev)
    z_move(q, 1, 0, 0, 1)
    z_move(q, 1, 0, 1, 1)
    for k in (2, 3):
        z_move(q, k, 0, 0, k + 2)
        z_move(q, k, 0, 1, k + 2)
    w_move(q, qo_half, x_recv.at[0], xdev)
    w_move(q, kv_half, sib_recv.at[0], sdev)
    w_move(q, qo_half, sib_recv.at[1], sdev)

    frame = slot_frame[q]
    level = levels[frame]
    t_a = timesteps[level].astype(F32)
    t_b = timesteps[jnp.maximum(level - 1, 0)].astype(F32)
    t_c = timesteps[jnp.maximum(level - 2, 0)].astype(F32)
    dsigma = [(t_b - t_a) * (1.0 / 1000.0), (t_c - t_b) * (1.0 / 1000.0)]

    row = lax.broadcasted_iota(jnp.int32, (16, FREQ // 2), 0)
    loads[5].wait()
    angle = jnp.where(row % 2 == 0, t_a, t_b) * OM[...]
    emb = jnp.concatenate([jnp.cos(angle), jnp.sin(angle)], axis=-1).astype(BF16)
    cols = SPACE * 48
    loads[3].wait()
    part = [
        jnp.dot(emb, MW[k], preferred_element_type=F32)[:8] for k in range(3)
    ]
    prow = lax.broadcasted_iota(jnp.int32, (8, cols), 0)
    packed = jnp.where(prow < 2, part[0], jnp.where(prow < 4, part[1], part[2]))
    MP[...] = packed
    MG[me] = packed
    for p in peers:
        send(MP, MG.at[me], mod_send, mod_recv, (q, p))

    loads[4].wait()
    x = HS[...].astype(F32)
    for g in range(GROUPS):
        XS[g, 0] = x[8 * g : 8 * g + 8, :HALF]
        XS[g, 1] = x[8 * g : 8 * g + 8, HALF:]

    def seed():
        w_wait(xp, kv_half, x_recv.at[16])
        for k in (0, 1):
            z_move(xp, k, 0, 0, k + 2)
            z_move(xp, k, 0, 1, k + 2)
        w_move(xp, kv_half, sib_recv.at[0], sdev)

    def relay(h, way, m):
        theirs = m in (2, 3)
        if h == 8 and theirs == (way == 0):
            return
        d = -h if way == 0 else h
        idx = xzq(d) if theirs else zq(d)
        k = (0, 1, 0, 1, 2, 3)[m]
        w_wait(idx, k, z_recv.at[way, h - 1, m])
        if h < 7 or (h == 7 and theirs == (way == 1)):
            z_move(idx, k, h, way, m)
        if m % 2 == 1:
            half = qo_half if m == 5 else kv_half
            if m == 5:
                w_move(idx, half, x_recv.at[h if way == 0 else 8 + h], xdev)
            w_move(idx, half, sib_recv.at[1 if m == 5 else 0], sdev)

    def take_x(j):
        idx = xp if j == 0 else (xzq(-j) if j <= 8 else xzq(j - 8))
        w_wait(idx, qo_half, x_recv.at[j])
        w_move(idx, qo_half, sib_recv.at[1], sdev)

    def finish_weights():
        wait(W.at[pl.ds(0, 16), pl.ds(0, 2), qo_half], sib_recv.at[1])

    def partner_weights():
        send(W.at[pl.ds(0, 32), c, 3], WX.at[pl.ds(0, 32), c], wx_send.at[0], wx_recv.at[0], odev)

    def share_partner_weights():
        own = WX.at[pl.ds(0, 32), c]
        wait(own, wx_recv.at[0])
        send(own, own, wx_send.at[1], wx_recv.at[1], sdev)

    def finish_partner_weights():
        wait(WX.at[pl.ds(0, 32), c], wx_recv.at[1])

    def spread_modulation():
        wait(MG.at[pl.ds(0, SPACE - 1)], mod_recv)
        for st in range(STEPS):
            for k in range(3):
                r = 2 * k + st
                for half in range(2):
                    vec = jnp.concatenate(
                        [MG[4 * half + j, r : r + 1, :] for j in range(4)], axis=-1
                    )
                    if k == 1:
                        vec = vec + 1.0
                    MODF[st, k, half] = jnp.broadcast_to(vec, (8, HALF))

    def g_move(st, g, at, rs, dev):
        ref = G.at[st, g, at]
        send(ref, ref, ag_send.at[st, g], rs, dev)

    def norm_send(st, g):
        left, right = XS[g, 0], XS[g, 1]
        mean = (
            jnp.sum(left, axis=-1, keepdims=True) + jnp.sum(right, axis=-1, keepdims=True)
        ) * (1.0 / (2 * HALF))
        left, right = left - mean, right - mean
        var = (
            jnp.sum(left * left, axis=-1, keepdims=True)
            + jnp.sum(right * right, axis=-1, keepdims=True)
        ) * (1.0 / (2 * HALF))
        inv = 1.0 / jnp.sqrt(var + 1e-6)
        left = left * inv * MODF[st, 1, 0] + MODF[st, 0, 0]
        right = right * inv * MODF[st, 1, 1] + MODF[st, 0, 1]
        G[st, g, slot] = jnp.concatenate([left, right], axis=0).astype(BF16)
        g_move(st, g, slot, agx_recv.at[st, g], hdev)
        g_move(st, g, slot, ag_recv.at[st, g], ydevs[0])
        g_move(st, g, slot, ag_recv.at[st, g], ydevs[1])
        g_move(st, g, slot, agy_recv.at[st, g], ydevs[2])

    def norm_pass(st, g):
        other = (1 - xh) * 4 + y
        wait(G.at[st, g, other], agx_recv.at[st, g])
        g_move(st, g, other, ag_recv.at[st, g], ydevs[0])
        g_move(st, g, other, ag_recv.at[st, g], ydevs[1])
        far = xh * 4 + (y + 2) % 4
        wait(G.at[st, g, far], agy_recv.at[st, g])
        g_move(st, g, far, ag_recv.at[st, g], hdev)

    def rms(values):
        parts = []
        for h in range(2):
            wide = values[:, h * HEAD_DIM : (h + 1) * HEAD_DIM]
            mean = jnp.mean(wide * wide, axis=-1, keepdims=True)
            parts.append(wide * (1.0 / jnp.sqrt(mean + 1e-6)))
        return jnp.concatenate(parts, axis=-1)

    def project(g, part_index):
        acc = None
        for j in range(4):
            term = jnp.dot(
                LHS[g, :, 768 * j : 768 * (j + 1)],
                W[8 * j : 8 * (j + 1), :, part_index].reshape(768, 256),
                preferred_element_type=F32,
            )
            acc = term if acc is None else acc + term
        return acc.astype(BF16)

    def kv_move(st, g, w, k, rs, dev, to):
        send(KV.at[st, g, w, k], KV.at[st, g, to, k], kv_send.at[st, g], rs, dev)

    def kv_pass(st, g, w, k, way):
        to = w + 2 if way else w - 2
        kv_move(st, g, w, k, kv_recv.at[st, g, to // 2, k], kv_down if way else kv_up, to)

    def kv_wait(st, g, w, k):
        wait(KV.at[st, g, w, k], kv_recv.at[st, g, w // 2, k])

    def sib_kv(st, g, w):
        to = w + 2 * c - 1
        send(KV.at[st, g, w], KV.at[st, g, to], kv_send.at[st, g], kvs_recv.at[st, g, to], sdev)

    def take_rows(st, g):
        wait(G.at[st, g, pl.ds(0, 5)], ag_recv.at[st, g])
        rows = G[st, g].astype(F32)
        LHS[g, :, :HALF] = rows[:, :8].reshape(64, HALF).astype(BF16)
        LHS[g, :, HALF:] = rows[:, 8:].reshape(64, HALF).astype(BF16)

    def project_kv(st, g):
        KV[st, g, 8, 0] = rms(project(g, 0).astype(F32)).astype(BF16)
        kv_pass(st, g, 8, 0, 0)
        kv_pass(st, g, 8, 0, 1)
        KV[st, g, 8, 1] = project(g, 1)
        kv_pass(st, g, 8, 1, 0)
        kv_pass(st, g, 8, 1, 1)
        sib_kv(st, g, 8)

    def project_q(st, g):
        hat = rms(project(g, 2).astype(F32)).astype(BF16).astype(F32)
        QS[g] = hat * (1.0 / math.sqrt(HEAD_DIM))

    def kv_relay(st, g, h):
        lo, hi = 8 - 2 * h, 8 + 2 * h
        if h < 4:
            for k in range(2):
                kv_wait(st, g, lo, k)
                kv_pass(st, g, lo, k, 0)
                kv_wait(st, g, hi, k)
                if h < 3:
                    kv_pass(st, g, hi, k, 1)
                else:

                    @pl.when(c == 0)
                    def _():
                        kv_pass(st, g, hi, k, 1)

            sib_kv(st, g, lo)
            sib_kv(st, g, hi)
        else:
            kv_wait(st, g, lo, 0)
            kv_wait(st, g, lo, 1)

            @pl.when(c == 0)
            def _():
                kv_wait(st, g, hi, 0)
                kv_wait(st, g, hi, 1)
                sib_kv(st, g, hi)

            @pl.when(c == 1)
            def _():
                sib_kv(st, g, lo)

    masks = []
    for w in range(16):
        f = frame + (w - 8)
        masks.append(jnp.where((f >= 0) & (f < FRAMES), 1.0, 0.0).astype(F32))

    def attend(st, g, places, first, last):
        for w in places:
            if w % 2 == 1:
                wait(KV.at[st, g, w], kvs_recv.at[st, g, w])

        def rows16(i, carry):
            at = pl.ds(pl.multiple_of(i * 16, 16), 16)
            for h in range(2):
                lanes = pl.ds(h * HEAD_DIM, HEAD_DIM)
                query = QS[g, at, lanes]
                if first:
                    num = jnp.zeros((16, HEAD_DIM), F32)
                    den = jnp.zeros((16, HEAD_DIM), F32)
                else:
                    num, den = NUM[g, at, lanes], DEN[g, at, lanes]
                for w in places:
                    key = KV[st, g, w, 0, at, lanes].astype(F32)
                    score = jnp.sum(query * key, axis=-1, keepdims=True)
                    e = jnp.exp(score) * masks[w]
                    den = den + e
                    num = num + e * KV[st, g, w, 1, at, lanes].astype(F32)
                if last:
                    ATT[st, g, i // 2, pl.ds(pl.multiple_of((i % 2) * 16, 16), 16), lanes] = (
                        num / den
                    ).astype(BF16)
                else:
                    NUM[g, at, lanes], DEN[g, at, lanes] = num, den
            return carry

        lax.fori_loop(0, 4, rows16, 0)

    def attend_near(st, g):
        attend(st, g, NEAR, True, False)

    def attend_far(st, g):
        attend(st, g, FAR, False, True)
        send(ATT.at[st, g, 1 - xh], ATX.at[st, g], at_send.at[st, g], at_recv.at[st, g], hdev)

    def out_send(st, g):
        wait(ATX.at[st, g], at_recv.at[st, g])
        own, other = ATT[st, g, xh], ATX[st, g]
        for j in range(2):
            pair = []
            for half in range(2):
                k = j + 2 * half
                total = None
                for rows, weight in (
                    (own, W[8 * k : 8 * (k + 1), :, 3]), (other, WX[8 * k : 8 * (k + 1)])
                ):
                    term = lax.dot_general(
                        rows, weight.reshape(768, 256), (((1,), (1,)), ((), ())),
                        preferred_element_type=F32,
                    )
                    total = term if total is None else total + term
                pair.append(total.reshape(4, 8, 768))
            PB[st, g, :, :, 768 * j : 768 * (j + 1)] = jnp.concatenate(pair, axis=1).astype(BF16)
        RB[st, g, y] = PB[st, g, y]
        for k, dev in zip((1, 3, 2), ydevs):
            send(
                PB.at[st, g, (y + k) % 4], RB.at[st, g, y],
                rs_send.at[st, g], rs_recv.at[st, g], dev,
            )

    def update(st, g):
        wait(RB.at[st, g, pl.ds(0, 3)], rs_recv.at[st, g])
        branch = jnp.sum(RB[st, g].astype(F32), axis=0)
        for half in range(2):
            cur = XS[g, half]
            vel = cur + MODF[st, 2, half] * branch[8 * half : 8 * half + 8]
            VO[st, 8 * g : 8 * g + 8, half * HALF : (half + 1) * HALF] = vel
            XS[g, half] = (cur + dsigma[st] * vel).astype(BF16).astype(F32)

    def queries_outputs(h):
        if h <= 8:
            for m in (4, 5):
                relay(h, 0, m)
                relay(h, 1, m)
        for j in X_TURNS[h]:
            take_x(j)

    for h in range(1, 9):
        for m in range(4):
            relay(h, 0, m)
            relay(h, 1, m)
            if h == 1 and m == 1:
                seed()
        queries_outputs(h)
        if h == 1:
            spread_modulation()
        if 2 <= h <= 4:
            norm_send(0, h - 2)
        if 5 <= h <= 7:
            norm_pass(0, h - 5)
    queries_outputs(9)
    partner_weights()
    wait(W.at[pl.ds(0, 16), pl.ds(0, 2), kv_half], sib_recv.at[0])

    def start(st, g):
        take_rows(st, g)
        project_kv(st, g)

    order = (
        [("start", g) for g in range(3)] + [("weights", 0)] + [("query", g) for g in range(3)]
        + [(h, g) for h in range(1, 4) for g in range(3)] + [("velocity", 0)]
        + ORDER
    )
    calls = {
        "start": start, "near": attend_near, "far": attend_far, "out": out_send,
        "query": lambda st, g: project_q(st, g),
        "weights": lambda st, g: st == 0 and finish_weights(),
        "share": lambda st, g: st == 0 and share_partner_weights(),
        "shared": lambda st, g: st == 0 and finish_partner_weights(),
    }
    for st in range(STEPS):
        for what, g in order:
            if what == "velocity":
                if st == 1:
                    vel_out[0, 0] = VO[0].astype(BF16)
            elif what in calls:
                calls[what](st, g)
            else:
                kv_relay(st, g, what)
        for g in range(GROUPS):
            update(st, g)
            if st + 1 < STEPS:
                norm_send(st + 1, g)
        if st + 1 < STEPS:
            for g in range(GROUPS):
                norm_pass(st + 1, g)

    vel_out[1, 0] = VO[1].astype(BF16)
    for g in range(GROUPS):
        for half in range(2):
            VO[0, 8 * g : 8 * g + 8, half * HALF : (half + 1) * HALF] = XS[g, half]
    lat_out[0] = VO[0].astype(BF16)

    wait(W.at[pl.ds(0, 31), 0], w_send.at[0])
    wait(W.at[pl.ds(0, 16)], w_send.at[1])
    for k in range(2):
        wait(WX.at[pl.ds(0, 32), c], wx_send.at[k])
    wait(MG.at[pl.ds(0, SPACE - 1)], mod_send)
    for st in range(STEPS):
        for g in range(GROUPS):
            wait(G.at[st, g, pl.ds(0, SPACE - 1)], ag_send.at[st, g])
            wait(ATX.at[st, g], at_send.at[st, g])
            wait(RB.at[st, g, pl.ds(0, 3)], rs_send.at[st, g])

            @pl.when(c == 0)
            def _():
                wait(KV.at[st, g, pl.ds(0, 16)], kv_send.at[st, g])

            @pl.when(c == 1)
            def _():
                wait(KV.at[st, g, pl.ds(0, 15)], kv_send.at[st, g])


def shards(hidden, qkv_weight, out_weight, mod_weight, slot_frame, levels, timesteps):
    half_freq = FREQ // 2
    omega = np.exp(-math.log(10000.0) * np.arange(half_freq) / half_freq).astype(np.float32)
    vmem = pl.BlockSpec(memory_space=pltpu.VMEM)
    hbm = pl.BlockSpec(memory_space=pltpu.HBM)
    smem = pl.BlockSpec(memory_space=pltpu.SMEM)
    dma = pltpu.SemaphoreType.DMA
    width = SPACE * 48
    return pl.pallas_call(
        kernel,
        name="denoise",
        out_shape=(
            jax.ShapeDtypeStruct((STEPS, 1, 24, 2 * HALF), BF16),
            jax.ShapeDtypeStruct((1, 24, 2 * HALF), BF16),
        ),
        in_specs=[hbm] * 5 + [smem] * 3,
        out_specs=(vmem, vmem),
        scratch_shapes=[
            pltpu.VMEM((FRAMES // 2, 2, 4, 48, 256), BF16),
            pltpu.VMEM((FRAMES // 2, 2, 48, 256), BF16),
            pltpu.VMEM((GROUPS, 2, 8, HALF), F32),
            pltpu.VMEM((8, width), F32),
            pltpu.VMEM((SPACE, 8, width), F32),
            pltpu.VMEM((STEPS, 3, 2, 8, HALF), F32),
            pltpu.VMEM((STEPS, GROUPS, SPACE, 16, HALF), BF16),
            pltpu.VMEM((GROUPS, 64, 2 * HALF), BF16),
            pltpu.VMEM((STEPS, GROUPS, 17, 2, 64, 256), BF16),
            pltpu.VMEM((GROUPS, 64, 256), F32),
            pltpu.VMEM((GROUPS, 64, 256), F32),
            pltpu.VMEM((GROUPS, 64, 256), F32),
            pltpu.VMEM((STEPS, GROUPS, 2, 32, 256), BF16),
            pltpu.VMEM((STEPS, GROUPS, 32, 256), BF16),
            pltpu.VMEM((STEPS, GROUPS, 4, 16, HALF), BF16),
            pltpu.VMEM((STEPS, GROUPS, 4, 16, HALF), BF16),
            pltpu.VMEM((STEPS, 24, 2 * HALF), F32),
            pltpu.VMEM((24, 2 * HALF), BF16),
            pltpu.VMEM((3, FREQ, width), BF16),
            pltpu.VMEM((1, FREQ // 2), F32),
            dma((6,)),
            dma((2,)),
            dma((2, 8, 6)),
            dma((17,)),
            dma((2,)),
            dma((2,)),
            dma((2,)),
            dma,
            dma,
            dma((STEPS, GROUPS)),
            dma((STEPS, GROUPS)),
            dma((STEPS, GROUPS)),
            dma((STEPS, GROUPS)),
            dma((STEPS, GROUPS)),
            dma((STEPS, GROUPS)),
            dma((STEPS, GROUPS)),
            dma((STEPS, GROUPS)),
            dma((STEPS, GROUPS)),
            dma((STEPS, GROUPS, 9, 2)),
            dma((STEPS, GROUPS, 16)),
        ],
        compiler_params=pltpu.CompilerParams(
            collective_id=0, has_side_effects=True, vmem_limit_bytes=63 * 1024 * 1024
        ),
    )(
        hidden, qkv_weight, out_weight, jnp.transpose(mod_weight, (1, 0, 2)), omega[None],
        slot_frame, levels, timesteps,
    )


def solution(mesh):
    in_specs = (
        P("queue", "space", None),
        P(None, "queue", "space"),
        P("queue", "space"),
        P(None, None, "space"),
        P(),
        P(),
        P(),
    )
    out_specs = (P(None, "queue", "space", None), P("queue", "space", None))
    return jax.shard_map(shards, mesh=mesh, in_specs=in_specs, out_specs=out_specs, check_vma=False)
```

```python
import functools
import math

import jax
import jax.numpy as jnp
import numpy as np
from jax import lax
from jax.experimental import pallas as pl
from jax.experimental.pallas import tpu as pltpu
from jax.sharding import PartitionSpec as P

MESH = pl.DeviceIdType.MESH
F32 = jnp.float32
BF16 = jnp.bfloat16
HEAD_DIM = 128
FREQ = 256
STEPS = 2
GROUPS = 3
HALF = 1536
SPACE = 8
ORDER = [("near", 0), ("near", 1), ("near", 2), (4, 0), (4, 1), (4, 2), ("share", 0), ("far", 0), ("far", 1),
         ("shared", 0), ("far", 2), ("out", 0), ("out", 1), ("out", 2)]
X_TURNS = {h: [] for h in range(1, 10)}
for _j in range(16):
    X_TURNS[(max(1, _j if _j <= 8 else _j - 8) + 1) if _j else 1].append(_j)
FRAMES = 64
FAR = (0, 1, 15)
NEAR = tuple(w for w in range(16) if w not in FAR)


def kernel(
    hid, qkvw, outw, modw, omega, slot_frame, levels, timesteps,
    vel_out, lat_out,
    W, WX, XS, MP, MG, MODF, G, LHS, KV, QS, NUM, DEN, ATT, ATX, PB, RB, VO, HS, MW, OM, in_sem,
    w_send, z_recv, x_recv, sib_recv, wx_send, wx_recv, mod_send, mod_recv,
    ag_send, ag_recv, agx_recv, agy_recv, at_send, at_recv, rs_send, rs_recv,
    kv_send, kv_recv, kvs_recv,
):
    q = lax.axis_index("queue")
    me = lax.axis_index("space")
    xl = q // 32
    z = (q % 32) // 2
    c = q % 2
    y, xh = me // 2, me % 2
    slot = xh * 4 + y
    sib = q + 1 - 2 * c
    xp = (q + 32) % FRAMES

    def zq(d):
        return xl * 32 + ((z + d + 16) % 16) * 2 + c

    def xzq(d):
        return (1 - xl) * 32 + ((z + d + 16) % 16) * 2 + c

    up_q = (q + 2) % FRAMES
    down_q = (q + FRAMES - 2) % FRAMES
    peers = [(me + k) % SPACE for k in range(1, SPACE)]
    ydevs = [(q, (me + 2 * k) % SPACE) for k in (1, 3, 2)]
    hdev = (q, me + 1 - 2 * xh)
    odev = (xp, me + 1 - 2 * xh)
    kv_up, kv_down = (up_q, me), (down_q, me)
    up, down = (zq(1), me), (zq(-1), me)
    xdev, sdev = (xp, me), (sib, me)

    def send(src, dst, ss, rs, dev):
        pltpu.make_async_remote_copy(
            src_ref=src, dst_ref=dst, send_sem=ss, recv_sem=rs,
            device_id=dev, device_id_type=MESH,
        ).start()

    def wait(ref, sem):
        pltpu.make_async_copy(ref, ref, sem).wait()

    barrier = pltpu.get_barrier_semaphore()
    targets = [up, down, xdev, sdev, odev, kv_up, kv_down] + [(q, p) for p in peers]
    for dev in targets:
        pl.semaphore_signal(barrier, inc=1, device_id=dev, device_id_type=MESH)

    loads = [
        pltpu.make_async_copy(qkvw.at[pl.ds(1, 2)], W.at[q // 2, c, pl.ds(0, 2)], in_sem.at[0]),
        pltpu.make_async_copy(qkvw.at[0], W.at[q // 2, c, 2], in_sem.at[1]),
        pltpu.make_async_copy(outw, W.at[q // 2, c, 3], in_sem.at[2]),
        pltpu.make_async_copy(modw, MW, in_sem.at[3]),
        pltpu.make_async_copy(hid.at[0], HS, in_sem.at[4]),
        pltpu.make_async_copy(omega, OM, in_sem.at[5]),
    ]
    for load in loads:
        load.start()

    kv_half, qo_half = pl.ds(0, 2), pl.ds(2, 2)

    def w_move(idx, half, rs, dev):
        ref = W.at[idx // 2, c, half]
        send(ref, ref, w_send.at[1 if dev is sdev else 0], rs, dev)

    def w_wait(idx, half, sem):
        wait(W.at[idx // 2, c, half], sem)

    def z_move(idx, k, h, way, m):
        w_move(idx, k, z_recv.at[way, h, m], down if way else up)

    for load in loads[:3]:
        load.wait()
    pl.semaphore_wait(barrier, len(targets))
    z_move(q, 0, 0, 0, 0)
    z_move(q, 0, 0, 1, 0)
    w_move(q, kv_half, x_recv.at[16], xdev)
    z_move(q, 1, 0, 0, 1)
    z_move(q, 1, 0, 1, 1)
    for k in (2, 3):
        z_move(q, k, 0, 0, k + 2)
        z_move(q, k, 0, 1, k + 2)
    w_move(q, qo_half, x_recv.at[0], xdev)
    w_move(q, kv_half, sib_recv.at[0], sdev)
    w_move(q, qo_half, sib_recv.at[1], sdev)

    frame = slot_frame[q]
    level = levels[frame]
    t_a = timesteps[level].astype(F32)
    t_b = timesteps[jnp.maximum(level - 1, 0)].astype(F32)
    t_c = timesteps[jnp.maximum(level - 2, 0)].astype(F32)
    dsigma = [(t_b - t_a) * (1.0 / 1000.0), (t_c - t_b) * (1.0 / 1000.0)]

    row = lax.broadcasted_iota(jnp.int32, (16, FREQ // 2), 0)
    loads[5].wait()
    angle = jnp.where(row % 2 == 0, t_a, t_b) * OM[...]
    emb = jnp.concatenate([jnp.cos(angle), jnp.sin(angle)], axis=-1).astype(BF16)
    cols = SPACE * 48
    loads[3].wait()
    part = [
        jnp.dot(emb, MW[k], preferred_element_type=F32)[:8] for k in range(3)
    ]
    prow = lax.broadcasted_iota(jnp.int32, (8, cols), 0)
    packed = jnp.where(prow < 2, part[0], jnp.where(prow < 4, part[1], part[2]))
    MP[...] = packed
    MG[me] = packed
    for p in peers:
        send(MP, MG.at[me], mod_send, mod_recv, (q, p))

    loads[4].wait()
    x = HS[...].astype(F32)
    for g in range(GROUPS):
        XS[g, 0] = x[8 * g : 8 * g + 8, :HALF]
        XS[g, 1] = x[8 * g : 8 * g + 8, HALF:]

    def seed():
        w_wait(xp, kv_half, x_recv.at[16])
        for k in (0, 1):
            z_move(xp, k, 0, 0, k + 2)
            z_move(xp, k, 0, 1, k + 2)
        w_move(xp, kv_half, sib_recv.at[0], sdev)

    def relay(h, way, m):
        theirs = m in (2, 3)
        if h == 8 and theirs == (way == 0):
            return
        d = -h if way == 0 else h
        idx = xzq(d) if theirs else zq(d)
        k = (0, 1, 0, 1, 2, 3)[m]
        w_wait(idx, k, z_recv.at[way, h - 1, m])
        if h < 7 or (h == 7 and theirs == (way == 1)):
            z_move(idx, k, h, way, m)
        if m % 2 == 1:
            half = qo_half if m == 5 else kv_half
            if m == 5:
                w_move(idx, half, x_recv.at[h if way == 0 else 8 + h], xdev)
            w_move(idx, half, sib_recv.at[1 if m == 5 else 0], sdev)

    def take_x(j):
        idx = xp if j == 0 else (xzq(-j) if j <= 8 else xzq(j - 8))
        w_wait(idx, qo_half, x_recv.at[j])
        w_move(idx, qo_half, sib_recv.at[1], sdev)

    def finish_weights():
        wait(W.at[pl.ds(0, 16), pl.ds(0, 2), qo_half], sib_recv.at[1])

    def partner_weights():
        send(W.at[pl.ds(0, 32), c, 3], WX.at[pl.ds(0, 32), c], wx_send.at[0], wx_recv.at[0], odev)

    def share_partner_weights():
        own = WX.at[pl.ds(0, 32), c]
        wait(own, wx_recv.at[0])
        send(own, own, wx_send.at[1], wx_recv.at[1], sdev)

    def finish_partner_weights():
        wait(WX.at[pl.ds(0, 32), c], wx_recv.at[1])

    def spread_modulation():
        wait(MG.at[pl.ds(0, SPACE - 1)], mod_recv)
        for st in range(STEPS):
            for k in range(3):
                r = 2 * k + st
                for half in range(2):
                    vec = jnp.concatenate(
                        [MG[4 * half + j, r : r + 1, :] for j in range(4)], axis=-1
                    )
                    if k == 1:
                        vec = vec + 1.0
                    MODF[st, k, half] = jnp.broadcast_to(vec, (8, HALF))

    def g_move(st, g, at, rs, dev):
        ref = G.at[st, g, at]
        send(ref, ref, ag_send.at[st, g], rs, dev)

    def norm_send(st, g):
        left, right = XS[g, 0], XS[g, 1]
        mean = (
            jnp.sum(left, axis=-1, keepdims=True) + jnp.sum(right, axis=-1, keepdims=True)
        ) * (1.0 / (2 * HALF))
        left, right = left - mean, right - mean
        var = (
            jnp.sum(left * left, axis=-1, keepdims=True)
            + jnp.sum(right * right, axis=-1, keepdims=True)
        ) * (1.0 / (2 * HALF))
        inv = 1.0 / jnp.sqrt(var + 1e-6)
        left = left * inv * MODF[st, 1, 0] + MODF[st, 0, 0]
        right = right * inv * MODF[st, 1, 1] + MODF[st, 0, 1]
        G[st, g, slot] = jnp.concatenate([left, right], axis=0).astype(BF16)
        g_move(st, g, slot, agx_recv.at[st, g], hdev)
        g_move(st, g, slot, agy_recv.at[st, g], ydevs[2])
        g_move(st, g, slot, ag_recv.at[st, g], ydevs[0])
        g_move(st, g, slot, ag_recv.at[st, g], ydevs[1])

    def norm_pass(st, g):
        other = (1 - xh) * 4 + y
        wait(G.at[st, g, other], agx_recv.at[st, g])
        g_move(st, g, other, ag_recv.at[st, g], ydevs[0])
        g_move(st, g, other, ag_recv.at[st, g], ydevs[1])
        far = xh * 4 + (y + 2) % 4
        wait(G.at[st, g, far], agy_recv.at[st, g])
        g_move(st, g, far, ag_recv.at[st, g], hdev)

    def rms(values):
        parts = []
        for h in range(2):
            wide = values[:, h * HEAD_DIM : (h + 1) * HEAD_DIM]
            mean = jnp.mean(wide * wide, axis=-1, keepdims=True)
            parts.append(wide * (1.0 / jnp.sqrt(mean + 1e-6)))
        return jnp.concatenate(parts, axis=-1)

    def project(g, part_index):
        acc = None
        for j in range(4):
            term = jnp.dot(
                LHS[g, :, 768 * j : 768 * (j + 1)],
                W[8 * j : 8 * (j + 1), :, part_index].reshape(768, 256),
                preferred_element_type=F32,
            )
            acc = term if acc is None else acc + term
        return acc.astype(BF16)

    def kv_move(st, g, w, k, rs, dev, to):
        send(KV.at[st, g, w, k], KV.at[st, g, to, k], kv_send.at[st, g], rs, dev)

    def kv_pass(st, g, w, k, way):
        to = w + 2 if way else w - 2
        kv_move(st, g, w, k, kv_recv.at[st, g, to // 2, k], kv_down if way else kv_up, to)

    def kv_wait(st, g, w, k):
        wait(KV.at[st, g, w, k], kv_recv.at[st, g, w // 2, k])

    def sib_kv(st, g, w):
        to = w + 2 * c - 1
        send(KV.at[st, g, w], KV.at[st, g, to], kv_send.at[st, g], kvs_recv.at[st, g, to], sdev)

    def take_rows(st, g):
        wait(G.at[st, g, pl.ds(0, 5)], ag_recv.at[st, g])
        rows = G[st, g].astype(F32)
        LHS[g, :, :HALF] = rows[:, :8].reshape(64, HALF).astype(BF16)
        LHS[g, :, HALF:] = rows[:, 8:].reshape(64, HALF).astype(BF16)

    def project_kv(st, g):
        KV[st, g, 8, 0] = rms(project(g, 0).astype(F32)).astype(BF16)
        kv_pass(st, g, 8, 0, 0)
        kv_pass(st, g, 8, 0, 1)
        KV[st, g, 8, 1] = project(g, 1)
        kv_pass(st, g, 8, 1, 0)
        kv_pass(st, g, 8, 1, 1)
        sib_kv(st, g, 8)

    def project_q(st, g):
        hat = rms(project(g, 2).astype(F32)).astype(BF16).astype(F32)
        QS[g] = hat * (1.0 / math.sqrt(HEAD_DIM))

    def kv_relay(st, g, h):
        lo, hi = 8 - 2 * h, 8 + 2 * h
        if h < 4:
            for k in range(2):
                kv_wait(st, g, lo, k)
                kv_pass(st, g, lo, k, 0)
                kv_wait(st, g, hi, k)
                if h < 3:
                    kv_pass(st, g, hi, k, 1)
                else:

                    @pl.when(c == 0)
                    def _():
                        kv_pass(st, g, hi, k, 1)

            sib_kv(st, g, lo)
            sib_kv(st, g, hi)
        else:
            kv_wait(st, g, lo, 0)
            kv_wait(st, g, lo, 1)

            @pl.when(c == 0)
            def _():
                kv_wait(st, g, hi, 0)
                kv_wait(st, g, hi, 1)
                sib_kv(st, g, hi)

            @pl.when(c == 1)
            def _():
                sib_kv(st, g, lo)

    masks = []
    for w in range(16):
        f = frame + (w - 8)
        masks.append(jnp.where((f >= 0) & (f < FRAMES), 1.0, 0.0).astype(F32))

    def attend(st, g, places, first, last):
        for w in places:
            if w % 2 == 1:
                wait(KV.at[st, g, w], kvs_recv.at[st, g, w])

        def rows16(i, carry):
            at = pl.ds(pl.multiple_of(i * 16, 16), 16)
            for h in range(2):
                lanes = pl.ds(h * HEAD_DIM, HEAD_DIM)
                query = QS[g, at, lanes]
                if first:
                    num = jnp.zeros((16, HEAD_DIM), F32)
                    den = jnp.zeros((16, HEAD_DIM), F32)
                else:
                    num, den = NUM[g, at, lanes], DEN[g, at, lanes]
                for w in places:
                    key = KV[st, g, w, 0, at, lanes].astype(F32)
                    score = jnp.sum(query * key, axis=-1, keepdims=True)
                    e = jnp.exp(score) * masks[w]
                    den = den + e
                    num = num + e * KV[st, g, w, 1, at, lanes].astype(F32)
                if last:
                    ATT[st, g, i // 2, pl.ds(pl.multiple_of((i % 2) * 16, 16), 16), lanes] = (
                        num / den
                    ).astype(BF16)
                else:
                    NUM[g, at, lanes], DEN[g, at, lanes] = num, den
            return carry

        lax.fori_loop(0, 4, rows16, 0)

    def attend_near(st, g):
        attend(st, g, NEAR, True, False)

    def attend_far(st, g):
        attend(st, g, FAR, False, True)
        send(ATT.at[st, g, 1 - xh], ATX.at[st, g], at_send.at[st, g], at_recv.at[st, g], hdev)

    def out_send(st, g):
        wait(ATX.at[st, g], at_recv.at[st, g])
        own, other = ATT[st, g, xh], ATX[st, g]
        for j in range(2):
            pair = []
            for half in range(2):
                k = j + 2 * half
                total = None
                for rows, weight in (
                    (own, W[8 * k : 8 * (k + 1), :, 3]), (other, WX[8 * k : 8 * (k + 1)])
                ):
                    term = lax.dot_general(
                        rows, weight.reshape(768, 256), (((1,), (1,)), ((), ())),
                        preferred_element_type=F32,
                    )
                    total = term if total is None else total + term
                pair.append(total.reshape(4, 8, 768))
            PB[st, g, :, :, 768 * j : 768 * (j + 1)] = jnp.concatenate(pair, axis=1).astype(BF16)
        RB[st, g, y] = PB[st, g, y]
        for k, dev in zip((2, 1, 3), (ydevs[2], ydevs[0], ydevs[1])):
            send(
                PB.at[st, g, (y + k) % 4], RB.at[st, g, y],
                rs_send.at[st, g], rs_recv.at[st, g], dev,
            )

    def update(st, g):
        wait(RB.at[st, g, pl.ds(0, 3)], rs_recv.at[st, g])
        branch = jnp.sum(RB[st, g].astype(F32), axis=0)
        for half in range(2):
            cur = XS[g, half]
            vel = cur + MODF[st, 2, half] * branch[8 * half : 8 * half + 8]
            VO[st, 8 * g : 8 * g + 8, half * HALF : (half + 1) * HALF] = vel
            XS[g, half] = (cur + dsigma[st] * vel).astype(BF16).astype(F32)

    def queries_outputs(h):
        if h <= 8:
            for m in (4, 5):
                relay(h, 0, m)
                relay(h, 1, m)
        for j in X_TURNS[h]:
            take_x(j)

    for h in range(1, 9):
        for m in range(4):
            relay(h, 0, m)
            relay(h, 1, m)
            if h == 1 and m == 1:
                seed()
        queries_outputs(h)
        if h == 1:
            spread_modulation()
        if 2 <= h <= 4:
            norm_send(0, h - 2)
        if 5 <= h <= 7:
            norm_pass(0, h - 5)
    queries_outputs(9)
    partner_weights()
    wait(W.at[pl.ds(0, 16), pl.ds(0, 2), kv_half], sib_recv.at[0])

    def start(st, g):
        take_rows(st, g)
        project_kv(st, g)

    order = (
        [("start", g) for g in range(3)] + [("weights", 0)] + [("query", g) for g in range(3)]
        + [(h, g) for h in range(1, 4) for g in range(3)] + [("velocity", 0)]
        + ORDER
    )
    calls = {
        "start": start, "near": attend_near, "far": attend_far, "out": out_send,
        "query": lambda st, g: project_q(st, g),
        "weights": lambda st, g: st == 0 and finish_weights(),
        "share": lambda st, g: st == 0 and share_partner_weights(),
        "shared": lambda st, g: st == 0 and finish_partner_weights(),
    }
    for st in range(STEPS):
        for what, g in order:
            if what == "velocity":
                if st == 1:
                    vel_out[0, 0] = VO[0].astype(BF16)
            elif what in calls:
                calls[what](st, g)
            else:
                kv_relay(st, g, what)
        for g in range(GROUPS):
            update(st, g)
            if st + 1 < STEPS:
                norm_send(st + 1, g)
        if st + 1 < STEPS:
            for g in range(GROUPS):
                norm_pass(st + 1, g)

    vel_out[1, 0] = VO[1].astype(BF16)
    for g in range(GROUPS):
        for half in range(2):
            VO[0, 8 * g : 8 * g + 8, half * HALF : (half + 1) * HALF] = XS[g, half]
    lat_out[0] = VO[0].astype(BF16)

    wait(W.at[pl.ds(0, 31), 0], w_send.at[0])
    wait(W.at[pl.ds(0, 16)], w_send.at[1])
    for k in range(2):
        wait(WX.at[pl.ds(0, 32), c], wx_send.at[k])
    wait(MG.at[pl.ds(0, SPACE - 1)], mod_send)
    for st in range(STEPS):
        for g in range(GROUPS):
            wait(G.at[st, g, pl.ds(0, SPACE - 1)], ag_send.at[st, g])
            wait(ATX.at[st, g], at_send.at[st, g])
            wait(RB.at[st, g, pl.ds(0, 3)], rs_send.at[st, g])

            @pl.when(c == 0)
            def _():
                wait(KV.at[st, g, pl.ds(0, 16)], kv_send.at[st, g])

            @pl.when(c == 1)
            def _():
                wait(KV.at[st, g, pl.ds(0, 15)], kv_send.at[st, g])


def shards(hidden, qkv_weight, out_weight, mod_weight, slot_frame, levels, timesteps):
    half_freq = FREQ // 2
    omega = np.exp(-math.log(10000.0) * np.arange(half_freq) / half_freq).astype(np.float32)
    vmem = pl.BlockSpec(memory_space=pltpu.VMEM)
    hbm = pl.BlockSpec(memory_space=pltpu.HBM)
    smem = pl.BlockSpec(memory_space=pltpu.SMEM)
    dma = pltpu.SemaphoreType.DMA
    width = SPACE * 48
    return pl.pallas_call(
        kernel,
        name="denoise",
        out_shape=(
            jax.ShapeDtypeStruct((STEPS, 1, 24, 2 * HALF), BF16),
            jax.ShapeDtypeStruct((1, 24, 2 * HALF), BF16),
        ),
        in_specs=[hbm] * 5 + [smem] * 3,
        out_specs=(vmem, vmem),
        scratch_shapes=[
            pltpu.VMEM((FRAMES // 2, 2, 4, 48, 256), BF16),
            pltpu.VMEM((FRAMES // 2, 2, 48, 256), BF16),
            pltpu.VMEM((GROUPS, 2, 8, HALF), F32),
            pltpu.VMEM((8, width), F32),
            pltpu.VMEM((SPACE, 8, width), F32),
            pltpu.VMEM((STEPS, 3, 2, 8, HALF), F32),
            pltpu.VMEM((STEPS, GROUPS, SPACE, 16, HALF), BF16),
            pltpu.VMEM((GROUPS, 64, 2 * HALF), BF16),
            pltpu.VMEM((STEPS, GROUPS, 17, 2, 64, 256), BF16),
            pltpu.VMEM((GROUPS, 64, 256), F32),
            pltpu.VMEM((GROUPS, 64, 256), F32),
            pltpu.VMEM((GROUPS, 64, 256), F32),
            pltpu.VMEM((STEPS, GROUPS, 2, 32, 256), BF16),
            pltpu.VMEM((STEPS, GROUPS, 32, 256), BF16),
            pltpu.VMEM((STEPS, GROUPS, 4, 16, HALF), BF16),
            pltpu.VMEM((STEPS, GROUPS, 4, 16, HALF), BF16),
            pltpu.VMEM((STEPS, 24, 2 * HALF), F32),
            pltpu.VMEM((24, 2 * HALF), BF16),
            pltpu.VMEM((3, FREQ, width), BF16),
            pltpu.VMEM((1, FREQ // 2), F32),
            dma((6,)),
            dma((2,)),
            dma((2, 8, 6)),
            dma((17,)),
            dma((2,)),
            dma((2,)),
            dma((2,)),
            dma,
            dma,
            dma((STEPS, GROUPS)),
            dma((STEPS, GROUPS)),
            dma((STEPS, GROUPS)),
            dma((STEPS, GROUPS)),
            dma((STEPS, GROUPS)),
            dma((STEPS, GROUPS)),
            dma((STEPS, GROUPS)),
            dma((STEPS, GROUPS)),
            dma((STEPS, GROUPS)),
            dma((STEPS, GROUPS, 9, 2)),
            dma((STEPS, GROUPS, 16)),
        ],
        compiler_params=pltpu.CompilerParams(
            collective_id=0, has_side_effects=True, vmem_limit_bytes=63 * 1024 * 1024
        ),
    )(
        hidden, qkv_weight, out_weight, jnp.transpose(mod_weight, (1, 0, 2)), omega[None],
        slot_frame, levels, timesteps,
    )


def solution(mesh):
    in_specs = (
        P("queue", "space", None),
        P(None, "queue", "space"),
        P("queue", "space"),
        P(None, None, "space"),
        P(),
        P(),
        P(),
    )
    out_specs = (P(None, "queue", "space", None), P("queue", "space", None))
    return jax.shard_map(shards, mesh=mesh, in_specs=in_specs, out_specs=out_specs, check_vma=False)
```
